32 devices in a mesh: dp: 16 (over z, y, core), space: 2 (over x).
Axes of the slice: x: 2, y: 2, z: 4, core: 2. Of those that a mesh axis runs over, the one named last changes fastest.
Arguments:
- volumes: bfloat16 [16, 16, 8, 16, 256], P('dp', 'space'), may hold values from -6 to 6
- cotangent: bfloat16 [16, 16, 8, 16, 256], P('dp', 'space'), may hold values from -6 to 6
- first_weight: float32 [256, 6912], P('dp'), may hold values from -0.078125 to 0.078125
- second_weight: float32 [256, 6912], P('dp'), may hold values from -0.078125 to 0.078125
- first_noise: float32 [256, 6912], P('dp'), may hold values from -6 to 6
- second_noise: float32 [256, 6912], P('dp'), may hold values from -6 to 6
Outputs:
- outputs: bfloat16 [16, 16, 8, 16, 256], P('dp', 'space')
- input_grads: bfloat16 [16, 16, 8, 16, 256], P('dp', 'space')
- new_first: float32 [256, 6912], P('dp')
- new_second: float32 [256, 6912], P('dp')
The draws below stay inside these ranges and needn't reach their ends.
All inputs are finite; a program needn't handle non-finite values.
Results may differ from the reference program's by a relative error of at most 0.014.
Values may be sent and summed in bfloat16 or wider, within the bound.
No kernel may reach another device: no remote copies, remote signals or barrier semaphores. Data moves between devices by JAX's collectives and lax.ppermute only.
A program may use at most 192 MiB of HBM per device.

```python
import math
import jax
import jax.numpy as jnp
from jax import lax

C = 256
TAPS = 27
H = 8
W = 16
CROPS = 16
DEPTH = 16
ALLCELLS = 32768


def strengthened(array, stream_key, source, target, shards_of, factor):
    def block_of(axis_at):
        return (jnp.arange(array.shape[axis_at]) // (array.shape[axis_at] // shards_of)).reshape((-1,) + (1,) * (array.ndim - 1 - axis_at))

    near = jax.random.permutation(stream_key, shards_of)[block_of(target)]
    far = (block_of(target) + shards_of // 2) % shards_of
    return jnp.where((block_of(source) == near) | (block_of(source) == far), factor * array, array)


def levels(rng, dims, shards, smallest, high):
    def one(position, shards_of):
        steps = jax.random.uniform(jax.random.fold_in(jax.random.fold_in(rng, 6), position), (shards_of,), jnp.float32, smallest / len(shards), high / len(shards))
        return jnp.repeat(jnp.exp(steps), dims[position] // shards_of).reshape((-1,) + (1,) * (len(dims) - position - 1))

    factor_of = one(*shards[0])
    for cut in shards[1:]:
        factor_of = factor_of * one(*cut)
    return factor_of


def centred(own_key, shape, spread, most, split=(), dtype=jnp.bfloat16):
    gain = levels(own_key, shape, split, -0.22, 0.18) if split else 1.0
    drawn = jax.random.normal(own_key, shape, jnp.float32) * spread * gain
    return jnp.minimum(jnp.maximum(drawn, -most), most).astype(dtype)


def heavy_noise(key, shape, scale, limit, split, heavy, kind=jnp.bfloat16):
    drawn = scale * jax.random.normal(key, shape, jnp.float32)
    if split:
        drawn = drawn * levels(key, shape, split, -0.22, 0.18)
    return jnp.clip(strengthened(drawn, jax.random.fold_in(key, 3), *heavy), -limit, limit).astype(kind)


def setup_inputs(seed: int = 0) -> dict:
    splits = jax.random.split(jax.random.key(seed), 7)
    return {
        "volumes": heavy_noise(splits[0], (CROPS, DEPTH, H, W, C), 1.0, 6.0, ((0, 16), (1, 2)), (0, 4, 16, 2.0)),
        "cotangent": centred(splits[1], (CROPS, DEPTH, H, W, C), 1.0, 6.0, ((0, 16), (1, 2))),
        "first_weight": centred(splits[2], (C, TAPS * C), (TAPS * C) ** -0.5, 0.078125, ((0, 16),), jnp.float32),
        "second_weight": centred(splits[3], (C, TAPS * C), (TAPS * C) ** -0.5, 0.078125, ((0, 16),), jnp.float32),
        "first_noise": centred(splits[4], (C, TAPS * C), 1.0, 6.0, ((0, 16),), jnp.float32),
        "second_noise": centred(splits[5], (C, TAPS * C), 1.0, 6.0, ((0, 16),), jnp.float32),
    }


NOISE_COEF = 0.25

def shifts():
    return [(along_z, along_y, along_x) for along_z in (-1, 0, 1) for along_y in (-1, 0, 1) for along_x in (-1, 0, 1)]

def window(padded, offset, direction, extent):
    starts = [1 + direction * amount for amount in offset]
    section = padded[starts[0]:starts[0] + extent[0], starts[1]:starts[1] + extent[1], starts[2]:starts[2] + extent[2]]
    return section.reshape(extent[0] * extent[1] * extent[2], padded.shape[-1])

def pad_cells(volume):
    return jnp.pad(volume, ((1, 1), (1, 1), (1, 1), (0, 0)))

def forward_conv(padded, weights, extent):
    channels = weights.shape[0]
    total = jnp.zeros((extent[0] * extent[1] * extent[2], channels), jnp.float32)
    for tap_index, offset in enumerate(shifts()):
        total = total + jnp.dot(window(padded, offset, 1, extent), weights[:, tap_index * channels:(tap_index + 1) * channels], preferred_element_type=jnp.float32)
    return total

def backward_conv(padded_grad, weights, extent):
    channels = weights.shape[0]
    total = jnp.zeros((extent[0] * extent[1] * extent[2], channels), jnp.float32)
    for tap_index, offset in enumerate(shifts()):
        total = total + lax.dot_general(window(padded_grad, offset, -1, extent), weights[:, tap_index * channels:(tap_index + 1) * channels], (((1,), (1,)), ((), ())), preferred_element_type=jnp.float32)
    return total

def weight_grad(padded, grad_rows, extent):
    blocks = [lax.dot_general(window(padded, offset, 1, extent), grad_rows, (((0,), (0,)), ((), ())), preferred_element_type=jnp.float32) for offset in shifts()]
    return jnp.concatenate(blocks, axis=1)

def reference(volumes, cotangent, first_weight, second_weight, first_noise, second_noise):
    first_bf = first_weight.astype(jnp.bfloat16)
    second_bf = second_weight.astype(jnp.bfloat16)
    extent = (DEPTH, H, W)

    def per_crop(carry, inputs):
        volume, upstream = inputs
        padded_in = pad_cells(volume)
        hidden = forward_conv(padded_in, first_bf, extent)
        active = jax.nn.silu(hidden).astype(jnp.bfloat16)
        padded_act = pad_cells(active.reshape(DEPTH, H, W, C))
        output = (volume.reshape(-1, C).astype(jnp.float32) + forward_conv(padded_act, second_bf, extent)).astype(jnp.bfloat16)
        upstream_rows = upstream.reshape(-1, C)
        act_grad = backward_conv(pad_cells(upstream), second_bf, extent)
        sigma = jax.nn.sigmoid(hidden)
        hidden_grad = (act_grad * sigma * (1.0 + hidden * (1.0 - sigma))).astype(jnp.bfloat16)
        input_grad = (upstream_rows.astype(jnp.float32) + backward_conv(pad_cells(hidden_grad.reshape(DEPTH, H, W, C)), first_bf, extent)).astype(jnp.bfloat16)
        first_total = carry[0] + weight_grad(padded_in, hidden_grad, extent)
        second_total = carry[1] + weight_grad(padded_act, upstream_rows, extent)
        return ((first_total, second_total), (output.reshape(DEPTH, H, W, C), input_grad.reshape(DEPTH, H, W, C)))
    zeros = jnp.zeros((C, TAPS * C), jnp.float32)
    totals, results = lax.scan(per_crop, (zeros, zeros), (volumes, cotangent))
    rate = 1.0 / math.sqrt(ALLCELLS)
    new_first = first_weight - rate * totals[0] + NOISE_COEF * first_noise
    new_second = second_weight - rate * totals[1] + NOISE_COEF * second_noise
    return (results[0], results[1], new_first, new_second)
```

```python
import functools
import math

import jax
import jax.numpy as jnp
from jax import lax
from jax.experimental import pallas as pl
from jax.experimental.pallas import tpu as pltpu
from jax.sharding import PartitionSpec as P

NOISE_COEF = 0.25
BF = jnp.bfloat16
F32 = jnp.float32
VMEM_LIMIT = 56 * 2**20


def dot(a, b):
    return jnp.dot(a, b, preferred_element_type=F32)


def dot_nt(a, b):
    return lax.dot_general(a, b, (((1,), (1,)), ((), ())), preferred_element_type=F32)


def reverse_bits(value, bits):
    total = jnp.zeros_like(value)
    for b in range(bits):
        total = total | (((value >> b) & 1) << (bits - 1 - b))
    return total


def relative_matrix(k, size, rows, bits):
    rel = lax.broadcasted_iota(jnp.int32, (size, size), 0)
    nat = lax.broadcasted_iota(jnp.int32, (size, size), 1)
    want = (k ^ reverse_bits(rel // rows, bits)) * rows + rel % rows
    return jnp.where(want == nat, 1.0, 0.0).astype(BF)


def member_matrix(h, channels, half):
    chan = lax.broadcasted_iota(jnp.int32, (channels, channels // 2), 0)
    hid = lax.broadcasted_iota(jnp.int32, (channels, channels // 2), 1)
    want = (hid // half) * (2 * half) + h * half + hid % half
    return jnp.where(want == chan, 1.0, 0.0).astype(BF)


def shift_matrix(cells, width):
    out = lax.broadcasted_iota(jnp.int32, (2 * cells, cells), 0)
    src = lax.broadcasted_iota(jnp.int32, (2 * cells, cells), 1)
    step = jnp.where(out < cells, -1, 1)
    cell = out % cells
    inside = (cell % width + step >= 0) & (cell % width + step < width)
    return jnp.where(inside & (src == cell + step), 1.0, 0.0).astype(BF)


def clear_border(t3, width, area):
    planes = t3.shape[1] - 2
    zero = jnp.zeros((3, planes + 2, width, t3.shape[3]), BF)
    t3[:, :, 0:width, :] = zero
    t3[:, :, width + area : 2 * width + area, :] = zero
    plane = jnp.zeros((3, area, t3.shape[3]), BF)
    t3[:, 0, width : width + area, :] = plane
    t3[:, planes + 1, width : width + area, :] = plane


def store_shifted(t3, plane, value, shifts, width, area):
    both = dot(shifts, value).astype(BF)
    channels = value.shape[1]
    rows = slice(width, width + area)
    t3[0, plane : plane + 2, rows, :] = both[: 2 * area].reshape(2, area, channels)
    t3[1, plane : plane + 2, rows, :] = value.reshape(2, area, channels)
    t3[2, plane : plane + 2, rows, :] = both[2 * area :].reshape(2, area, channels)


def window(t3, c, plane, count, b, width, area):
    block = t3[c, pl.ds(plane, count), b * width : b * width + area, :]
    return block.reshape(count * area, t3.shape[3])


def weights_kernel(half, idx, first, second, w1, w2):
    h = idx[1]
    channels = 2 * w1.shape[1] // 27
    hid = channels // 2
    select = member_matrix(h, channels, half)
    for a in range(3):
        for bc in range(9):
            t = a * 9 + bc
            u = bc * 3 + a
            taps = first[:, t * channels : (t + 1) * channels].astype(BF)
            w1[:, u * hid : (u + 1) * hid] = dot(taps, select).astype(BF)
    w2[...] = jnp.where(h == 0, second[0:half, :], second[half : 2 * half, :]).astype(BF)


def spread_kernel(dims, relative, idx, own, other, t3, *rest):
    slab, width, area, rows, bits = dims
    k, h = idx[0], idx[1]
    channels = t3.shape[3]
    clear_border(t3, width, area)
    shifts = shift_matrix(2 * area, width)
    if relative:
        matrix = relative_matrix(k, channels, rows, bits)
    for pair in range(slab):
        plane = 2 * pair
        member, inside = plane // slab, plane % slab
        mine = own[inside : inside + 2].reshape(2 * area, channels)
        theirs = other[inside : inside + 2].reshape(2 * area, channels)
        value = jnp.where(h == member, mine, theirs)
        if relative:
            rest[0][:, plane * area : (plane + 2) * area] = dot_nt(matrix, value).astype(BF)
            value = dot_nt(value, matrix).astype(BF)
        store_shifted(t3, plane + 1, value, shifts, width, area)


def planes_of(halo, planes):
    if halo:
        return [(p, 2) for p in range(0, planes + 2, 2)]
    return [(1 + p, planes // 2) for p in range(0, planes, planes // 2)]


def hidden_kernel(dims, halo, idx, x3, w1, a3, at, slope, z):
    slab, width, area, rows, bits = dims
    k = idx[0]
    hid = w1.shape[1] // 27
    planes = 2 * slab
    for plane, count in planes_of(halo, planes):
        total = None
        for b in range(3):
            for c in range(3):
                u = b * 3 + c
                part = dot(window(x3, c, plane, count, b, width, area), w1[:, u * 3 * hid : (u + 1) * 3 * hid])
                total = part if total is None else total + part
        z[plane : plane + count] = total.reshape(count, area, 3 * hid)
    if not halo:
        z[0] = jnp.zeros((area, 3 * hid), F32)
        z[planes + 1] = jnp.zeros((area, 3 * hid), F32)
    clear_border(a3, width, area)
    shifts = shift_matrix(2 * area, width)
    matrix = relative_matrix(k, hid, rows // 2, bits)
    for d in range(0, planes, 2):
        hidden = z[d : d + 2, :, 0:hid] + z[d + 1 : d + 3, :, hid : 2 * hid] + z[d + 2 : d + 4, :, 2 * hid : 3 * hid]
        hidden = hidden.reshape(2 * area, hid)
        sigma = jax.nn.sigmoid(hidden)
        active = (hidden * sigma).astype(BF)
        grad = (sigma * (1.0 + hidden * (1.0 - sigma))).astype(BF)
        at[:, d * area : (d + 2) * area] = dot_nt(matrix, active).astype(BF)
        slope[d : d + 2] = dot_nt(grad, matrix).astype(BF).reshape(2, area, hid)
        store_shifted(a3, d + 1, dot_nt(active, matrix).astype(BF), shifts, width, area)


def second_grad_kernel(dims, at, c3, keep, send):
    slab, width, area, rows, bits = dims
    channels = c3.shape[3]
    half = keep.shape[0]
    for a in range(3):
        for b in range(3):
            for c in range(3):
                t = (a * 3 + b) * 3 + c
                right = window(c3, 2 - c, 2 - a, 2 * slab, 2 - b, width, area)
                value = dot(at[...], right).astype(BF)
                keep[:, t * channels : (t + 1) * channels] = value[:half]
                send[:, t * channels : (t + 1) * channels] = value[half:]


def hidden_grad_kernel(dims, halo, idx, c3, w2, slope, g3, z):
    slab, width, area, rows, bits = dims
    k = idx[0]
    hid = w2.shape[0]
    channels = c3.shape[3]
    planes = 2 * slab
    for plane, count in planes_of(halo, planes):
        total = None
        for b in range(3):
            for c in range(3):
                taps = [(a * 3 + b) * 3 + c for a in range(3)]
                right = jnp.concatenate([w2[:, t * channels : (t + 1) * channels] for t in taps], axis=0)
                part = dot_nt(window(c3, 2 - c, plane, count, 2 - b, width, area), right)
                total = part if total is None else total + part
        z[plane : plane + count] = total.reshape(count, area, 3 * hid)
    if not halo:
        z[0] = jnp.zeros((area, 3 * hid), F32)
        z[planes + 1] = jnp.zeros((area, 3 * hid), F32)
    clear_border(g3, width, area)
    shifts = shift_matrix(2 * area, width)
    matrix = relative_matrix(k, hid, rows // 2, bits)
    for d in range(0, planes, 2):
        grad = z[d + 2 : d + 4, :, 0:hid] + z[d + 1 : d + 3, :, hid : 2 * hid] + z[d : d + 2, :, 2 * hid : 3 * hid]
        grad = grad.reshape(2 * area, hid)
        value = (grad * slope[d : d + 2].reshape(2 * area, hid).astype(F32)).astype(BF)
        store_shifted(g3, d + 1, dot(value, matrix).astype(BF), shifts, width, area)


def first_grad_kernel(dims, xt, g3, keep, send):
    slab, width, area, rows, bits = dims
    hid = g3.shape[3]
    half = keep.shape[0]
    taps = [(a, b, c) for b in range(3) for c in range(3) for a in range(3)]
    for u in range(0, 27, 2):
        blocks = [window(g3, 2 - c, 2 - a, 2 * slab, 2 - b, width, area) for a, b, c in taps[u : u + 2]]
        right = jnp.concatenate(blocks, axis=1)
        value = dot(xt[...], right).astype(BF)
        keep[:, u * hid : (u + len(blocks)) * hid] = value[:half]
        send[:, u * hid : (u + len(blocks)) * hid] = value[half:]


def outputs_kernel(dims, idx, a3, w2, base, keep, send):
    slab, width, area, rows, bits = dims
    h = idx[1]
    channels = w2.shape[1] // 27
    taps = [(a, b, c) for a in range(3) for b in range(3) for c in range(3)]
    for mine in (False, True):
        start = (h if mine else 1 - h) * slab
        total = None
        for t in range(0, 27, 2):
            left = [window(a3, c, start + a, slab, b, width, area) for a, b, c in taps[t : t + 2]]
            right = [w2[:, v * channels : (v + 1) * channels] for v in range(t, t + len(left))]
            part = dot(jnp.concatenate(left, axis=1), jnp.concatenate(right, axis=0))
            total = part if total is None else total + part
        total = total.reshape(slab, area, channels)
        if mine:
            keep[...] = base[...].astype(F32) + total
        else:
            send[...] = total.astype(BF)


def input_grads_kernel(dims, idx, g3, w1, base, keep, send):
    slab, width, area, rows, bits = dims
    k, h = idx[0], idx[1]
    hid = w1.shape[1] // 27
    channels = w1.shape[0]
    matrix = relative_matrix(k, channels, rows, bits)
    taps = [(a, b, c) for b in range(3) for c in range(3) for a in range(3)]
    for mine in (False, True):
        start = (h if mine else 1 - h) * slab
        total = None
        for u in range(0, 27, 2):
            left = [window(g3, 2 - c, start + 2 - a, slab, 2 - b, width, area) for a, b, c in taps[u : u + 2]]
            part = dot_nt(jnp.concatenate(left, axis=1), w1[:, u * hid : (u + len(left)) * hid])
            total = part if total is None else total + part
        high = total.astype(BF)
        natural = dot(high, matrix)
        if mine:
            low = (total - high.astype(F32)).astype(BF)
            natural = natural + dot(low, matrix)
            keep[...] = base[...].astype(F32) + natural.reshape(slab, area, channels)
        else:
            send[...] = natural.astype(BF).reshape(slab, area, channels)


def update_kernel(half, rate, idx, own1, other1, own2, other2, first, second, noise1, noise2, new1, new2):
    h = idx[1]
    hid = own1.shape[1] // 27
    channels = 2 * hid
    mine = member_matrix(h, channels, half)
    theirs = member_matrix(1 - h, channels, half)
    for a in range(3):
        for bc in range(9):
            t = a * 9 + bc
            u = bc * 3 + a
            cols = slice(t * channels, (t + 1) * channels)
            part = slice(u * hid, (u + 1) * hid)
            grad = dot_nt(own1[:, part], mine) + dot_nt(other1[:, part], theirs)
            new1[:, cols] = first[:, cols] - rate * grad + NOISE_COEF * noise1[:, cols]
    mine2 = own2[...].astype(F32)
    theirs2 = other2[...].astype(F32)
    low = jnp.where(h == 0, mine2, theirs2)
    high = jnp.where(h == 0, theirs2, mine2)
    new2[0:half, :] = second[0:half, :] - rate * low + NOISE_COEF * noise2[0:half, :]
    new2[half : 2 * half, :] = (
        second[half : 2 * half, :] - rate * high + NOISE_COEF * noise2[half : 2 * half, :]
    )


def run(kernel, args, outs, name, flops, scalars=1, scratch=()):
    moved = sum(math.prod(a.shape) * a.dtype.itemsize for a in (*args, *outs))
    smem = pl.BlockSpec(memory_space=pltpu.SMEM)
    vmem = pl.BlockSpec(memory_space=pltpu.VMEM)
    return pl.pallas_call(
        kernel,
        out_shape=tuple(outs),
        in_specs=[smem] * scalars + [vmem] * (len(args) - scalars),
        out_specs=tuple([vmem] * len(outs)),
        scratch_shapes=list(scratch),
        compiler_params=pltpu.CompilerParams(vmem_limit_bytes=VMEM_LIMIT),
        cost_estimate=pl.CostEstimate(flops=flops, bytes_accessed=moved, transcendentals=0),
        name=name,
    )(*args)


def trade(array, axis, bit):
    size = lax.axis_size(axis)
    return lax.ppermute(array, axis, [(i, i ^ bit) for i in range(size)])


def gather(array, bits):
    for b in range(bits - 1, -1, -1):
        array = jnp.concatenate([array, trade(array, "dp", 1 << b)], axis=0)
    return array


def add(a, b):
    return (a.astype(F32) + b.astype(F32)).astype(BF)


def scatter(keep, send, bits):
    for b in range(bits):
        came = trade(send, "dp", 1 << b)
        if b == bits - 1:
            keep = add(keep, came)
        else:
            half = keep.shape[0] // 2
            keep, send = add(keep[:half], came[:half]), add(keep[half:], came[half:])
    pairs = lax.axis_size("space") // 2
    step = 1
    while step < pairs:
        keep = add(keep, trade(keep, "space", 2 * step))
        step *= 2
    return keep


def with_halo(t3):
    size = lax.axis_size("space")
    if size == 2:
        return t3
    last = t3.shape[1] - 1
    before = lax.ppermute(t3[:, last - 1], "space", [(i, i + 2) for i in range(size - 2)])
    after = lax.ppermute(t3[:, 1], "space", [(i + 2, i) for i in range(size - 2)])
    return t3.at[:, 0].set(before).at[:, last].set(after)


def body(volumes, cotangent, first_weight, second_weight, first_noise, second_noise):
    _, slab, height, width, channels = volumes.shape
    area = height * width
    hid = channels // 2
    devices = lax.axis_size("dp")
    members = lax.axis_size("space")
    rows = channels // devices
    half = rows // 2
    bits = devices.bit_length() - 1
    dims = (slab, width, area, rows, bits)
    halo = members > 2
    planes = 2 * slab
    cells = planes * area
    heavy = 2 * cells * 27 * channels * hid
    idx = jnp.stack([lax.axis_index("dp"), lax.axis_index("space") % 2]).astype(jnp.int32)
    volume = volumes.reshape(slab, area, channels)
    upstream = cotangent.reshape(slab, area, channels)
    shape = jax.ShapeDtypeStruct

    def padded(count):
        return shape((3, planes + 2, area + 2 * width, count), BF)

    w1, w2 = run(
        functools.partial(weights_kernel, half),
        (idx, first_weight, second_weight),
        (shape((rows, 27 * hid), BF), shape((half, 27 * channels), BF)),
        "weights",
        2 * rows * 27 * channels * hid,
    )
    w1 = gather(w1, bits)
    other_volume = trade(volume, "space", 1)
    x3, xt = run(
        functools.partial(spread_kernel, dims, True),
        (idx, volume, other_volume),
        (padded(channels), shape((channels, cells), BF)),
        "spread_volumes",
        8 * cells * channels * channels,
    )
    x3 = with_halo(x3)
    other_upstream = trade(upstream, "space", 1)
    (c3,) = run(
        functools.partial(spread_kernel, dims, False),
        (idx, upstream, other_upstream),
        (padded(channels),),
        "spread_cotangent",
        4 * cells * channels * channels,
    )
    c3 = with_halo(c3)
    w2 = gather(w2, bits)
    scratch = [pltpu.VMEM((planes + 2, area, 3 * hid), F32)]
    a3, at, slope = run(
        functools.partial(hidden_kernel, dims, halo),
        (idx, x3, w1),
        (padded(hid), shape((hid, cells), BF), shape((planes, area, hid), BF)),
        "hidden",
        heavy,
        scratch=scratch,
    )
    a3 = with_halo(a3)
    keep2, send2 = run(
        functools.partial(second_grad_kernel, dims),
        (at, c3),
        (shape((hid // 2, 27 * channels), BF),) * 2,
        "second_grad",
        heavy,
        scalars=0,
    )
    share2 = scatter(keep2, send2, bits)
    (g3,) = run(
        functools.partial(hidden_grad_kernel, dims, halo),
        (idx, c3, w2, slope),
        (padded(hid),),
        "hidden_grad",
        heavy,
        scratch=scratch,
    )
    g3 = with_halo(g3)
    keep1, send1 = run(
        functools.partial(first_grad_kernel, dims),
        (xt, g3),
        (shape((channels // 2, 27 * hid), BF),) * 2,
        "first_grad",
        heavy,
        scalars=0,
    )
    share1 = scatter(keep1, send1, bits)
    parts = (shape((slab, area, channels), F32), shape((slab, area, channels), BF))
    own_out, send_out = run(
        functools.partial(outputs_kernel, dims), (idx, a3, w2, volume), parts, "outputs", heavy
    )
    came_out = trade(send_out, "space", 1)
    own_in, send_in = run(
        functools.partial(input_grads_kernel, dims), (idx, g3, w1, upstream), parts, "input_grads", heavy
    )
    came_in = trade(send_in, "space", 1)
    outputs = (own_out + came_out.astype(F32)).astype(BF).reshape(volumes.shape)
    input_grads = (own_in + came_in.astype(F32)).astype(BF).reshape(volumes.shape)
    other2 = trade(share2, "space", 1)
    other1 = trade(share1, "space", 1)
    rate = 1.0 / math.sqrt(slab * area * devices * members)
    new_first, new_second = run(
        functools.partial(update_kernel, half, rate),
        (idx, share1, other1, share2, other2, first_weight, second_weight, first_noise, second_noise),
        (shape(first_weight.shape, F32),) * 2,
        "update",
        4 * rows * 27 * channels * hid,
    )
    return (outputs, input_grads, new_first, new_second)


def solution(mesh):
    cells = P("dp", "space", None, None, None)
    rows = P("dp", None)
    return jax.shard_map(
        body,
        mesh=mesh,
        in_specs=(cells, cells, rows, rows, rows, rows),
        out_specs=(cells, cells, rows, rows),
        check_vma=False,
    )
```

```python
import functools
import math

import jax
import jax.numpy as jnp
from jax import lax
from jax.experimental import pallas as pl
from jax.experimental.pallas import tpu as pltpu
from jax.sharding import PartitionSpec as P

NOISE_COEF = 0.25
BF = jnp.bfloat16
F32 = jnp.float32
SPARE = 8 * 2**20
NONE, SHORTER, ALL = 1, 10**10, 10**11


def dot(a, b):
    return jnp.dot(a, b, preferred_element_type=F32)


def dot_nt(a, b):
    return lax.dot_general(a, b, (((1,), (1,)), ((), ())), preferred_element_type=F32)


def over(value, size):
    return value >> (size.bit_length() - 1)


def within(value, size):
    return value & (size - 1)


def reverse_bits(value, bits):
    total = jnp.zeros_like(value)
    for b in range(bits):
        total = total | (((value >> b) & 1) << (bits - 1 - b))
    return total


def relative_matrix(k, size, rows, bits):
    rel = lax.broadcasted_iota(jnp.int32, (size, size), 0)
    nat = lax.broadcasted_iota(jnp.int32, (size, size), 1)
    want = (k ^ reverse_bits(over(rel, rows), bits)) * rows + within(rel, rows)
    return jnp.where(want == nat, 1.0, 0.0).astype(BF)


def member_matrix(h, channels, half):
    chan = lax.broadcasted_iota(jnp.int32, (channels, channels // 2), 0)
    hid = lax.broadcasted_iota(jnp.int32, (channels, channels // 2), 1)
    want = over(hid, half) * (2 * half) + h * half + within(hid, half)
    return jnp.where(want == chan, 1.0, 0.0).astype(BF)


def shift_matrix(cells, width):
    out = lax.broadcasted_iota(jnp.int32, (2 * cells, cells), 0)
    src = lax.broadcasted_iota(jnp.int32, (2 * cells, cells), 1)
    step = jnp.where(out < cells, -1, 1)
    cell = within(out, cells)
    place = within(cell, width) + step
    inside = (place >= 0) & (place < width)
    return jnp.where(inside & (src == cell + step), 1.0, 0.0).astype(BF)


def clear_border(t3, width, area):
    planes = t3.shape[1] - 2
    zero = jnp.zeros((3, planes + 2, width, t3.shape[3]), BF)
    t3[:, :, 0:width, :] = zero
    t3[:, :, width + area : 2 * width + area, :] = zero
    plane = jnp.zeros((3, area, t3.shape[3]), BF)
    t3[:, 0, width : width + area, :] = plane
    t3[:, planes + 1, width : width + area, :] = plane


def store_shifted(t3, plane, value, shifts, width, area):
    both = dot(shifts, value).astype(BF)
    channels = value.shape[1]
    rows = slice(width, width + area)
    t3[0, plane : plane + 2, rows, :] = both[: 2 * area].reshape(2, area, channels)
    t3[1, plane : plane + 2, rows, :] = value.reshape(2, area, channels)
    t3[2, plane : plane + 2, rows, :] = both[2 * area :].reshape(2, area, channels)


def window(t3, c, plane, count, b, width, area):
    block = t3[c, pl.ds(plane, count), b * width : b * width + area, :]
    return block.reshape(count * area, t3.shape[3])


def base_kernel(weight, noise, base):
    base[...] = weight[...] + NOISE_COEF * noise[...]


def second_rows_kernel(half, idx, second, w2):
    w2[...] = jnp.where(idx[1] == 0, second[0:half, :], second[half : 2 * half, :]).astype(BF)


def first_columns_kernel(half, idx, first, w1):
    h = idx[1]
    channels = 2 * w1.shape[1] // 27
    hid = channels // 2
    select = member_matrix(h, channels, half)
    for a in range(3):
        for bc in range(9):
            t = a * 9 + bc
            u = bc * 3 + a
            taps = first[:, t * channels : (t + 1) * channels].astype(BF)
            w1[:, u * hid : (u + 1) * hid] = dot(taps, select).astype(BF)


def spread_kernel(dims, relative, idx, own, other, t3, *rest):
    slab, width, area, rows, bits = dims
    k, h = idx[0], idx[1]
    channels = t3.shape[3]
    clear_border(t3, width, area)
    shifts = shift_matrix(2 * area, width)
    if relative:
        matrix = relative_matrix(k, channels, rows, bits)
    for pair in range(slab):
        plane = 2 * pair
        member, inside = plane // slab, plane % slab
        mine = own[inside : inside + 2].reshape(2 * area, channels)
        theirs = other[inside : inside + 2].reshape(2 * area, channels)
        value = jnp.where(h == member, mine, theirs)
        if relative:
            rest[0][:, plane * area : (plane + 2) * area] = dot_nt(matrix, value).astype(BF)
        store_shifted(t3, plane + 1, value, shifts, width, area)


def planes_of(halo, planes):
    if halo:
        return [(p, 2) for p in range(0, planes + 2, 2)]
    return [(1 + p, planes // 2) for p in range(0, planes, planes // 2)]


def hidden_kernel(dims, halo, idx, x3, w1, a3, at, slope, z):
    slab, width, area, rows, bits = dims
    k = idx[0]
    hid = w1.shape[1] // 27
    planes = 2 * slab
    for plane, count in planes_of(halo, planes):
        total = None
        for b in range(3):
            for c in range(3):
                u = b * 3 + c
                part = dot(window(x3, c, plane, count, b, width, area), w1[:, u * 3 * hid : (u + 1) * 3 * hid])
                total = part if total is None else total + part
        z[plane : plane + count] = total.reshape(count, area, 3 * hid)
    if not halo:
        z[0] = jnp.zeros((area, 3 * hid), F32)
        z[planes + 1] = jnp.zeros((area, 3 * hid), F32)
    clear_border(a3, width, area)
    shifts = shift_matrix(2 * area, width)
    matrix = relative_matrix(k, hid, rows // 2, bits)
    for d in range(0, planes, 2):
        hidden = z[d : d + 2, :, 0:hid] + z[d + 1 : d + 3, :, hid : 2 * hid] + z[d + 2 : d + 4, :, 2 * hid : 3 * hid]
        hidden = hidden.reshape(2 * area, hid)
        sigma = jax.nn.sigmoid(hidden)
        active = (hidden * sigma).astype(BF)
        grad = (sigma * (1.0 + hidden * (1.0 - sigma))).astype(BF)
        at[:, d * area : (d + 2) * area] = dot_nt(matrix, active).astype(BF)
        slope[d : d + 2] = dot_nt(grad, matrix).astype(BF).reshape(2, area, hid)
        store_shifted(a3, d + 1, dot_nt(active, matrix).astype(BF), shifts, width, area)


def second_grad_kernel(dims, at, c3, keep, send):
    slab, width, area, rows, bits = dims
    channels = c3.shape[3]
    half = keep.shape[0]
    for a in range(3):
        for b in range(3):
            for c in range(3):
                t = (a * 3 + b) * 3 + c
                right = window(c3, 2 - c, 2 - a, 2 * slab, 2 - b, width, area)
                value = dot(at[...], right).astype(BF)
                keep[:, t * channels : (t + 1) * channels] = value[:half]
                send[:, t * channels : (t + 1) * channels] = value[half:]


def hidden_grad_kernel(dims, halo, idx, c3, w2, slope, g3, z):
    slab, width, area, rows, bits = dims
    k = idx[0]
    hid = w2.shape[0]
    channels = c3.shape[3]
    planes = 2 * slab
    for plane, count in planes_of(halo, planes):
        total = None
        for b in range(3):
            for c in range(3):
                taps = [(a * 3 + b) * 3 + c for a in range(3)]
                right = jnp.concatenate([w2[:, t * channels : (t + 1) * channels] for t in taps], axis=0)
                part = dot_nt(window(c3, 2 - c, plane, count, 2 - b, width, area), right)
                total = part if total is None else total + part
        z[plane : plane + count] = total.reshape(count, area, 3 * hid)
    if not halo:
        z[0] = jnp.zeros((area, 3 * hid), F32)
        z[planes + 1] = jnp.zeros((area, 3 * hid), F32)
    clear_border(g3, width, area)
    shifts = shift_matrix(2 * area, width)
    matrix = relative_matrix(k, hid, rows // 2, bits)
    for d in range(0, planes, 2):
        grad = z[d + 2 : d + 4, :, 0:hid] + z[d + 1 : d + 3, :, hid : 2 * hid] + z[d : d + 2, :, 2 * hid : 3 * hid]
        grad = grad.reshape(2 * area, hid)
        value = (grad * slope[d : d + 2].reshape(2 * area, hid).astype(F32)).astype(BF)
        store_shifted(g3, d + 1, dot(value, matrix).astype(BF), shifts, width, area)


def first_grad_kernel(dims, xt, g3, keep, send):
    slab, width, area, rows, bits = dims
    hid = g3.shape[3]
    half = keep.shape[0]
    taps = [(a, b, c) for b in range(3) for c in range(3) for a in range(3)]
    for u in range(0, 27, 2):
        blocks = [window(g3, 2 - c, 2 - a, 2 * slab, 2 - b, width, area) for a, b, c in taps[u : u + 2]]
        right = jnp.concatenate(blocks, axis=1)
        value = dot(xt[...], right).astype(BF)
        keep[:, u * hid : (u + len(blocks)) * hid] = value[:half]
        send[:, u * hid : (u + len(blocks)) * hid] = value[half:]


def outputs_kernel(dims, mine, idx, a3, w2, *refs):
    slab, width, area, rows, bits = dims
    channels = w2.shape[1] // 27
    taps = [(a, b, c) for a in range(3) for b in range(3) for c in range(3)]
    start = (idx[1] if mine else 1 - idx[1]) * slab
    total = None
    for t in range(0, 27, 2):
        left = [window(a3, c, start + a, slab, b, width, area) for a, b, c in taps[t : t + 2]]
        right = [w2[:, v * channels : (v + 1) * channels] for v in range(t, t + len(left))]
        part = dot(jnp.concatenate(left, axis=1), jnp.concatenate(right, axis=0))
        total = part if total is None else total + part
    total = total.reshape(slab, area, channels)
    if mine:
        total = refs[0][...].astype(F32) + total
    refs[-1][...] = total.astype(refs[-1].dtype)


def input_grads_kernel(dims, mine, idx, g3, w1, *refs):
    slab, width, area, rows, bits = dims
    hid = w1.shape[1] // 27
    taps = [(a, b, c) for b in range(3) for c in range(3) for a in range(3)]
    start = (idx[1] if mine else 1 - idx[1]) * slab
    total = None
    for u in range(0, 27, 2):
        left = [window(g3, 2 - c, start + 2 - a, slab, 2 - b, width, area) for a, b, c in taps[u : u + 2]]
        part = dot_nt(jnp.concatenate(left, axis=1), w1[:, u * hid : (u + len(left)) * hid])
        total = part if total is None else total + part
    total = total.reshape(slab, area, w1.shape[0])
    if mine:
        total = refs[0][...].astype(F32) + total
    refs[-1][...] = total.astype(refs[-1].dtype)


def update_first_kernel(half, rate, idx, own, other, base, new):
    h = idx[1]
    hid = own.shape[1] // 27
    channels = 2 * hid
    mine = member_matrix(h, channels, half)
    theirs = member_matrix(1 - h, channels, half)
    for a in range(3):
        for bc in range(9):
            t = a * 9 + bc
            u = bc * 3 + a
            cols = slice(t * channels, (t + 1) * channels)
            part = slice(u * hid, (u + 1) * hid)
            grad = dot_nt(own[:, part], mine) + dot_nt(other[:, part], theirs)
            new[:, cols] = base[:, cols] - rate * grad


def update_second_kernel(half, rate, idx, own, other, base, new):
    h = idx[1]
    mine = own[...].astype(F32)
    theirs = other[...].astype(F32)
    for member in range(2):
        grad = jnp.where(h == member, mine, theirs)
        rows = slice(member * half, (member + 1) * half)
        new[rows, :] = base[rows, :] - rate * grad


def finish_kernel(own, came, out):
    out[...] = (own[...] + came[...].astype(F32)).astype(BF)


def run(kernel, args, outs, name, cost, scalars=1, scratch=(), after=()):
    moved = sum(math.prod(a.shape) * a.dtype.itemsize for a in (*args, *outs))
    room = moved + sum(math.prod(a.shape) * a.dtype.itemsize for a in scratch)
    smem = pl.BlockSpec(memory_space=pltpu.SMEM)
    vmem = pl.BlockSpec(memory_space=pltpu.VMEM)
    anywhere = pl.BlockSpec(memory_space=pl.ANY)
    count = len(args)

    def entry(*refs):
        kernel(*refs[:count], *refs[count + len(after) :])

    return pl.pallas_call(
        entry,
        out_shape=tuple(outs),
        in_specs=[smem] * scalars + [vmem] * (count - scalars) + [anywhere] * len(after),
        out_specs=tuple([vmem] * len(outs)),
        scratch_shapes=list(scratch),
        compiler_params=pltpu.CompilerParams(vmem_limit_bytes=room + SPARE),
        cost_estimate=pl.CostEstimate(flops=cost, bytes_accessed=1, transcendentals=0),
        name=name,
    )(*args, *after)


def trade(array, axis, bit):
    size = lax.axis_size(axis)
    return lax.ppermute(array, axis, [(i, i ^ bit) for i in range(size)])


def join_kernel(*refs):
    row = 0
    for ref in refs[:-1]:
        refs[-1][row : row + ref.shape[0], :] = ref[...]
        row += ref.shape[0]


def join(parts, name, after=(), cost=NONE):
    total = jax.ShapeDtypeStruct((sum(p.shape[0] for p in parts), parts[0].shape[1]), BF)
    return run(join_kernel, tuple(parts), (total,), name, cost, scalars=0, after=after)[0]


def place_kernel(rows, bits, idx, *refs):
    q = 0
    for ref in refs[:-1]:
        for row in range(0, ref.shape[0], rows):
            owner = idx[0] ^ int(f"{q:0{bits}b}"[::-1], 2)
            refs[-1][pl.ds(pl.multiple_of(owner * rows, rows), rows), :] = ref[row : row + rows, :]
            q += 1


def fold_kernel(count, *refs):
    total = refs[0][...].astype(F32)
    for ref in refs[1:count]:
        total = total + ref[...].astype(F32)
    total = total.astype(BF)
    row = 0
    for out in refs[count:]:
        out[...] = total[row : row + out.shape[0]]
        row += out.shape[0]


def fold(parts, name, split=1, after=(), cost=NONE):
    rows, columns = parts[0].shape
    out = jax.ShapeDtypeStruct((rows // split, columns), BF)
    kernel = functools.partial(fold_kernel, len(parts))
    return run(kernel, tuple(parts), (out,) * split, name, cost, scalars=0, after=after)


def add(a, b):
    return (a.astype(F32) + b.astype(F32)).astype(BF)


def over_pairs(share):
    pairs = lax.axis_size("space") // 2
    step = 1
    while step < pairs:
        share = add(share, trade(share, "space", 2 * step))
        step *= 2
    return share


def with_halo(t3):
    size = lax.axis_size("space")
    if size == 2:
        return t3
    last = t3.shape[1] - 1
    before = lax.ppermute(t3[:, last - 1], "space", [(i, i + 2) for i in range(size - 2)])
    after = lax.ppermute(t3[:, 1], "space", [(i + 2, i) for i in range(size - 2)])
    return t3.at[:, 0].set(before).at[:, last].set(after)


def body(volumes, cotangent, first_weight, second_weight, first_noise, second_noise):
    _, slab, height, width, channels = volumes.shape
    area = height * width
    hid = channels // 2
    devices = lax.axis_size("dp")
    members = lax.axis_size("space")
    rows = channels // devices
    half = rows // 2
    bits = devices.bit_length() - 1
    dims = (slab, width, area, rows, bits)
    halo = members > 2
    planes = 2 * slab
    cells = planes * area
    idx = jnp.stack([lax.axis_index("dp"), lax.axis_index("space") % 2]).astype(jnp.int32)
    volume = volumes.reshape(slab, area, channels)
    upstream = cotangent.reshape(slab, area, channels)
    shape = jax.ShapeDtypeStruct

    def padded(count):
        return shape((3, planes + 2, area + 2 * width, count), BF)

    core, near, line, far = 1, 2, 4, 8

    other_volume = trade(volume, "space", 1)
    (w1,) = run(
        functools.partial(first_columns_kernel, half),
        (idx, first_weight),
        (shape((rows, 27 * hid), BF),),
        "first_columns",
        NONE,
    )
    w1 = join((w1, trade(w1, "dp", far)), "join1")
    (w2,) = run(
        functools.partial(second_rows_kernel, half),
        (idx, second_weight),
        (shape((half, 27 * channels), BF),),
        "second_rows",
        SHORTER,
        after=(w1,),
    )
    line1, near1 = trade(w1, "dp", line), trade(w1, "dp", near)
    w1 = join((w1, line1, near1), "join1", after=(w2,))
    both1 = trade(line1, "dp", near)
    far2 = trade(w2, "dp", far)
    x3, xt = run(
        functools.partial(spread_kernel, dims, True),
        (idx, volume, other_volume),
        (padded(channels), shape((channels, cells), BF)),
        "spread_volumes",
        ALL,
        after=(w1,),
    )
    x3 = with_halo(x3)
    sum_of = shape(first_weight.shape, F32)
    (base1,) = run(base_kernel, (first_weight, first_noise), (sum_of,), "base1", NONE, scalars=0, after=(xt,))
    w1 = join((w1, both1), "join1", after=(base1,))
    core1 = trade(w1, "dp", core)
    w2 = join((w2, far2), "join2", after=(w1,), cost=ALL)
    line2, near2 = trade(w2, "dp", line), trade(w2, "dp", near)
    (w1,) = run(
        functools.partial(place_kernel, rows, bits),
        (idx, w1, core1),
        (shape((channels, 27 * hid), BF),),
        "place1",
        NONE,
        after=(w2,),
    )
    scratch = [pltpu.VMEM((planes + 2, area, 3 * hid), F32)]
    a3, at, slope = run(
        functools.partial(hidden_kernel, dims, halo),
        (idx, x3, w1),
        (padded(hid), shape((hid, cells), BF), shape((planes, area, hid), BF)),
        "hidden",
        SHORTER,
        scratch=scratch,
    )
    a3 = with_halo(a3)

    w2 = join((w2, line2, near2), "join2", after=(slope,))
    line2 = join((line2,), "join2", after=(slope,))
    both2 = trade(line2, "dp", near)
    other_upstream = trade(upstream, "space", 1)
    (c3,) = run(
        functools.partial(spread_kernel, dims, False),
        (idx, upstream, other_upstream),
        (padded(channels),),
        "spread_cotangent",
        ALL,
        after=(w2,),
    )
    c3 = with_halo(c3)
    keep2, send2 = run(
        functools.partial(second_grad_kernel, dims),
        (at, c3),
        (shape((hid // 2, 27 * channels), BF),) * 2,
        "second_grad",
        NONE,
        scalars=0,
    )
    w2 = join((w2, both2), "join2", after=(keep2,), cost=ALL)
    core2 = trade(w2, "dp", core)
    q01, q23, q45, q67 = fold((keep2, trade(send2, "dp", core)), "fold2", split=4, after=(w2,), cost=ALL)
    w2 = join((w2, core2), "join2", after=(q01,))
    (g3,) = run(
        functools.partial(hidden_grad_kernel, dims, halo),
        (idx, c3, w2, slope),
        (padded(hid),),
        "hidden_grad",
        ALL,
        scratch=scratch,
    )
    g3 = with_halo(g3)

    (q23,) = fold((q23, trade(q67, "dp", near)), "fold2", after=(g3,))
    line2, near2 = trade(q23, "dp", line), trade(join((q45,), "join2", after=(g3,)), "dp", near)
    keep1, send1 = run(
        functools.partial(first_grad_kernel, dims),
        (xt, g3),
        (shape((channels // 2, 27 * hid), BF),) * 2,
        "first_grad",
        ALL,
        scalars=0,
        after=(q23,),
    )
    q0, q1 = fold((q01, line2, near2), "fold2", split=2, after=(keep1,), cost=ALL)
    p01, p23, p45, p67 = fold((keep1, trade(send1, "dp", core)), "fold1", split=4, after=(q0,))
    near1 = trade(p67, "dp", near)
    part, whole = shape((slab, area, channels), BF), shape((slab, area, channels), F32)
    (send_out,) = run(
        functools.partial(outputs_kernel, dims, False), (idx, a3, w2), (part,), "outputs_send", ALL, after=(p01,)
    )
    came_out = trade(send_out, "space", 1)
    (p23,) = fold((p23, near1), "fold1", after=(send_out,))
    line1, near1 = trade(p23, "dp", line), trade(join((p45,), "join1", after=(send_out,)), "dp", near)
    far2 = trade(join((q1,), "join2", after=(p23,)), "dp", far)
    (send_in,) = run(
        functools.partial(input_grads_kernel, dims, False), (idx, g3, w1), (part,), "input_grads_send", ALL, after=(p23,)
    )
    came_in = trade(send_in, "space", 1)
    p0, p1 = fold((p01, line1, near1), "fold1", split=2, after=(send_in,))
    (own_out,) = run(
        functools.partial(outputs_kernel, dims, True), (idx, a3, w2, volume), (whole,), "outputs", SHORTER, after=(p0,)
    )
    (share2,) = fold((q0, far2), "fold2", after=(own_out,))
    share2 = over_pairs(share2)
    other2 = trade(share2, "space", 1)
    (own_in,) = run(
        functools.partial(input_grads_kernel, dims, True),
        (idx, g3, w1, upstream),
        (whole,),
        "input_grads",
        NONE,
        after=(share2,),
    )
    (share1,) = fold((p0, trade(p1, "dp", far)), "fold1", after=(own_in,))
    share1 = over_pairs(share1)
    other1 = trade(share1, "space", 1)
    (base2,) = run(base_kernel, (second_weight, second_noise), (sum_of,), "base2", NONE, scalars=0, after=(own_out,))
    (outputs,) = run(finish_kernel, (own_out, came_out), (part,), "finish", NONE, scalars=0, after=(share1, base2))
    rate = 1.0 / math.sqrt(slab * area * devices * members)
    (new_second,) = run(
        functools.partial(update_second_kernel, half, rate),
        (idx, share2, other2, base2),
        (sum_of,),
        "update_second",
        NONE,
        after=(outputs,),
    )
    (new_first,) = run(
        functools.partial(update_first_kernel, half, rate),
        (idx, share1, other1, base1),
        (sum_of,),
        "update_first",
        NONE,
        after=(new_second,),
    )
    (input_grads,) = run(finish_kernel, (own_in, came_in), (part,), "finish", NONE, scalars=0, after=(new_first,))
    return (outputs.reshape(volumes.shape), input_grads.reshape(volumes.shape), new_first, new_second)


def solution(mesh):
    cells = P("dp", "space", None, None, None)
    rows = P("dp", None)
    return jax.shard_map(
        body,
        mesh=mesh,
        in_specs=(cells, cells, rows, rows, rows, rows),
        out_specs=(cells, cells, rows, rows),
        check_vma=False,
    )
```

```python
import functools
import math

import jax
import jax.numpy as jnp
from jax import lax
from jax.experimental import pallas as pl
from jax.experimental.pallas import tpu as pltpu
from jax.sharding import PartitionSpec as P

NOISE_COEF = 0.25
BF = jnp.bfloat16
F32 = jnp.float32
SPARE, SPARE_HEAVY = 2**20, 5 * 2**20
NONE, SHORTER, ALL = 1, 10**10, 10**11


def dot(a, b):
    return jnp.dot(a, b, preferred_element_type=F32)


def dot_nt(a, b):
    return lax.dot_general(a, b, (((1,), (1,)), ((), ())), preferred_element_type=F32)


def over(value, size):
    return value >> (size.bit_length() - 1)


def within(value, size):
    return value & (size - 1)


def reverse_bits(value, bits):
    total = jnp.zeros_like(value)
    for b in range(bits):
        total = total | (((value >> b) & 1) << (bits - 1 - b))
    return total


def relative_matrix(k, size, rows, bits):
    rel = lax.broadcasted_iota(jnp.int32, (size, size), 0)
    nat = lax.broadcasted_iota(jnp.int32, (size, size), 1)
    want = (k ^ reverse_bits(over(rel, rows), bits)) * rows + within(rel, rows)
    return jnp.where(want == nat, 1.0, 0.0).astype(BF)


def member_matrix(h, channels, half):
    chan = lax.broadcasted_iota(jnp.int32, (channels, channels // 2), 0)
    hid = lax.broadcasted_iota(jnp.int32, (channels, channels // 2), 1)
    want = over(hid, half) * (2 * half) + h * half + within(hid, half)
    return jnp.where(want == chan, 1.0, 0.0).astype(BF)


def shift_matrix(cells, width):
    out = lax.broadcasted_iota(jnp.int32, (2 * cells, cells), 0)
    src = lax.broadcasted_iota(jnp.int32, (2 * cells, cells), 1)
    step = jnp.where(out < cells, -1, 1)
    cell = within(out, cells)
    place = within(cell, width) + step
    inside = (place >= 0) & (place < width)
    return jnp.where(inside & (src == cell + step), 1.0, 0.0).astype(BF)


def clear_border(t3, width, area):
    planes = t3.shape[1] - 2
    zero = jnp.zeros((3, planes + 2, width, t3.shape[3]), BF)
    t3[:, :, 0:width, :] = zero
    t3[:, :, width + area : 2 * width + area, :] = zero
    plane = jnp.zeros((3, area, t3.shape[3]), BF)
    t3[:, 0, width : width + area, :] = plane
    t3[:, planes + 1, width : width + area, :] = plane


def store_shifted(t3, plane, value, shifts, width, area):
    both = dot(shifts, value).astype(BF)
    channels = value.shape[1]
    rows = slice(width, width + area)
    t3[0, plane : plane + 2, rows, :] = both[: 2 * area].reshape(2, area, channels)
    t3[1, plane : plane + 2, rows, :] = value.reshape(2, area, channels)
    t3[2, plane : plane + 2, rows, :] = both[2 * area :].reshape(2, area, channels)


def window(t3, c, plane, count, b, width, area):
    block = t3[c, pl.ds(plane, count), b * width : b * width + area, :]
    return block.reshape(count * area, t3.shape[3])


def base_kernel(weight, noise, base):
    base[...] = weight[...] + NOISE_COEF * noise[...]


def second_rows_kernel(half, idx, second, w2):
    w2[...] = jnp.where(idx[1] == 0, second[0:half, :], second[half : 2 * half, :]).astype(BF)


def first_columns_kernel(half, idx, first, w1):
    h = idx[1]
    channels = 2 * w1.shape[1] // 27
    hid = channels // 2
    select = member_matrix(h, channels, half)
    for a in range(3):
        for bc in range(9):
            t = a * 9 + bc
            u = bc * 3 + a
            taps = first[:, t * channels : (t + 1) * channels].astype(BF)
            w1[:, u * hid : (u + 1) * hid] = dot(taps, select).astype(BF)


def spread_kernel(dims, relative, idx, own, other, t3, *rest):
    slab, width, area, rows, bits = dims
    k, h = idx[0], idx[1]
    channels = t3.shape[3]
    clear_border(t3, width, area)
    shifts = shift_matrix(2 * area, width)
    if relative:
        matrix = relative_matrix(k, channels, rows, bits)
    for pair in range(slab):
        plane = 2 * pair
        member, inside = plane // slab, plane % slab
        mine = own[inside : inside + 2].reshape(2 * area, channels)
        theirs = other[inside : inside + 2].reshape(2 * area, channels)
        value = jnp.where(h == member, mine, theirs)
        if relative:
            rest[0][:, plane * area : (plane + 2) * area] = dot_nt(matrix, value).astype(BF)
        store_shifted(t3, plane + 1, value, shifts, width, area)


def planes_of(halo, planes):
    if halo:
        return [(p, 2) for p in range(0, planes + 2, 2)]
    return [(1 + p, planes // 2) for p in range(0, planes, planes // 2)]


def hidden_kernel(dims, halo, idx, x3, w1, a3, at, slope, z):
    slab, width, area, rows, bits = dims
    k = idx[0]
    hid = w1.shape[1] // 27
    planes = 2 * slab
    for plane, count in planes_of(halo, planes):
        total = None
        for b in range(3):
            for c in range(3):
                u = b * 3 + c
                part = dot(window(x3, c, plane, count, b, width, area), w1[:, u * 3 * hid : (u + 1) * 3 * hid])
                total = part if total is None else total + part
        z[plane : plane + count] = total.reshape(count, area, 3 * hid)
    if not halo:
        z[0] = jnp.zeros((area, 3 * hid), F32)
        z[planes + 1] = jnp.zeros((area, 3 * hid), F32)
    clear_border(a3, width, area)
    shifts = shift_matrix(2 * area, width)
    matrix = relative_matrix(k, hid, rows // 2, bits)
    for d in range(0, planes, 2):
        hidden = z[d : d + 2, :, 0:hid] + z[d + 1 : d + 3, :, hid : 2 * hid] + z[d + 2 : d + 4, :, 2 * hid : 3 * hid]
        hidden = hidden.reshape(2 * area, hid)
        sigma = jax.nn.sigmoid(hidden)
        active = (hidden * sigma).astype(BF)
        grad = (sigma * (1.0 + hidden * (1.0 - sigma))).astype(BF)
        at[:, d * area : (d + 2) * area] = dot_nt(matrix, active).astype(BF)
        slope[d : d + 2] = dot_nt(grad, matrix).astype(BF).reshape(2, area, hid)
        store_shifted(a3, d + 1, dot_nt(active, matrix).astype(BF), shifts, width, area)


def second_grad_kernel(dims, at, c3, keep, send):
    slab, width, area, rows, bits = dims
    channels = c3.shape[3]
    half = keep.shape[0]
    for a in range(3):
        for b in range(3):
            for c in range(3):
                t = (a * 3 + b) * 3 + c
                right = window(c3, 2 - c, 2 - a, 2 * slab, 2 - b, width, area)
                value = dot(at[...], right).astype(BF)
                keep[:, t * channels : (t + 1) * channels] = value[:half]
                send[:, t * channels : (t + 1) * channels] = value[half:]


def hidden_grad_kernel(dims, halo, idx, c3, w2, slope, g3, z):
    slab, width, area, rows, bits = dims
    k = idx[0]
    hid = w2.shape[0]
    channels = c3.shape[3]
    planes = 2 * slab
    for plane, count in planes_of(halo, planes):
        total = None
        for b in range(3):
            for c in range(3):
                taps = [(a * 3 + b) * 3 + c for a in range(3)]
                right = jnp.concatenate([w2[:, t * channels : (t + 1) * channels] for t in taps], axis=0)
                part = dot_nt(window(c3, 2 - c, plane, count, 2 - b, width, area), right)
                total = part if total is None else total + part
        z[plane : plane + count] = total.reshape(count, area, 3 * hid)
    if not halo:
        z[0] = jnp.zeros((area, 3 * hid), F32)
        z[planes + 1] = jnp.zeros((area, 3 * hid), F32)
    clear_border(g3, width, area)
    shifts = shift_matrix(2 * area, width)
    matrix = relative_matrix(k, hid, rows // 2, bits)
    for d in range(0, planes, 2):
        grad = z[d + 2 : d + 4, :, 0:hid] + z[d + 1 : d + 3, :, hid : 2 * hid] + z[d : d + 2, :, 2 * hid : 3 * hid]
        grad = grad.reshape(2 * area, hid)
        value = (grad * slope[d : d + 2].reshape(2 * area, hid).astype(F32)).astype(BF)
        store_shifted(g3, d + 1, dot(value, matrix).astype(BF), shifts, width, area)


def first_grad_kernel(dims, xt, g3, keep, send):
    slab, width, area, rows, bits = dims
    hid = g3.shape[3]
    half = keep.shape[0]
    taps = [(a, b, c) for b in range(3) for c in range(3) for a in range(3)]
    for u in range(0, 27, 2):
        blocks = [window(g3, 2 - c, 2 - a, 2 * slab, 2 - b, width, area) for a, b, c in taps[u : u + 2]]
        right = jnp.concatenate(blocks, axis=1)
        value = dot(xt[...], right).astype(BF)
        keep[:, u * hid : (u + len(blocks)) * hid] = value[:half]
        send[:, u * hid : (u + len(blocks)) * hid] = value[half:]


def outputs_kernel(dims, mine, idx, a3, w2, *refs):
    slab, width, area, rows, bits = dims
    channels = w2.shape[1] // 27
    taps = [(a, b, c) for a in range(3) for b in range(3) for c in range(3)]
    start = (idx[1] if mine else 1 - idx[1]) * slab
    total = None
    for t in range(0, 27, 2):
        left = [window(a3, c, start + a, slab, b, width, area) for a, b, c in taps[t : t + 2]]
        right = [w2[:, v * channels : (v + 1) * channels] for v in range(t, t + len(left))]
        part = dot(jnp.concatenate(left, axis=1), jnp.concatenate(right, axis=0))
        total = part if total is None else total + part
    total = total.reshape(slab, area, channels)
    if mine:
        total = refs[0][...].astype(F32) + total
    refs[-1][...] = total.astype(refs[-1].dtype)


def input_grads_kernel(dims, mine, idx, g3, w1, *refs):
    slab, width, area, rows, bits = dims
    hid = w1.shape[1] // 27
    taps = [(a, b, c) for b in range(3) for c in range(3) for a in range(3)]
    start = (idx[1] if mine else 1 - idx[1]) * slab
    total = None
    for u in range(0, 27, 2):
        left = [window(g3, 2 - c, start + 2 - a, slab, 2 - b, width, area) for a, b, c in taps[u : u + 2]]
        part = dot_nt(jnp.concatenate(left, axis=1), w1[:, u * hid : (u + len(left)) * hid])
        total = part if total is None else total + part
    total = total.reshape(slab, area, w1.shape[0])
    if mine:
        total = refs[0][...].astype(F32) + total
    refs[-1][...] = total.astype(refs[-1].dtype)


def update_first_kernel(half, rate, idx, own, other, base, new):
    h = idx[1]
    hid = own.shape[1] // 27
    channels = 2 * hid
    rows = own.shape[0]
    spread = jnp.concatenate([member_matrix(h, channels, half), member_matrix(1 - h, channels, half)], axis=1)
    both = [jnp.concatenate([r[:, u * hid : (u + 1) * hid] for u in range(27)], axis=0) for r in (own, other)]
    grad = dot_nt(jnp.concatenate(both, axis=1), spread)
    for a in range(3):
        for bc in range(9):
            t, u = a * 9 + bc, bc * 3 + a
            cols = slice(t * channels, (t + 1) * channels)
            new[:, cols] = base[:, cols] - rate * grad[u * rows : (u + 1) * rows]


def update_second_kernel(half, rate, idx, own, other, base, new):
    h = idx[1]
    mine = own[...].astype(F32)
    theirs = other[...].astype(F32)
    for member in range(2):
        grad = jnp.where(h == member, mine, theirs)
        rows = slice(member * half, (member + 1) * half)
        new[rows, :] = base[rows, :] - rate * grad


def finish_kernel(own, came, out):
    out[...] = (own[...] + came[...].astype(F32)).astype(BF)


def run(kernel, args, outs, name, cost, scalars=1, scratch=(), after=()):
    moved = sum(math.prod(a.shape) * a.dtype.itemsize for a in (*args, *outs))
    room = moved + sum(math.prod(a.shape) * a.dtype.itemsize for a in scratch)
    smem = pl.BlockSpec(memory_space=pltpu.SMEM)
    vmem = pl.BlockSpec(memory_space=pltpu.VMEM)
    anywhere = pl.BlockSpec(memory_space=pl.ANY)
    count = len(args)

    def entry(*refs):
        kernel(*refs[:count], *refs[count + len(after) :])

    return pl.pallas_call(
        entry,
        out_shape=tuple(outs),
        in_specs=[smem] * scalars + [vmem] * (count - scalars) + [anywhere] * len(after),
        out_specs=tuple([vmem] * len(outs)),
        scratch_shapes=list(scratch),
        compiler_params=pltpu.CompilerParams(vmem_limit_bytes=room + (SPARE if room < 5 * 2**20 else SPARE_HEAVY)),
        cost_estimate=pl.CostEstimate(flops=cost, bytes_accessed=1, transcendentals=0),
        name=name,
    )(*args, *after)


def trade(array, axis, bit):
    size = lax.axis_size(axis)
    return lax.ppermute(array, axis, [(i, i ^ bit) for i in range(size)])


def join_kernel(*refs):
    row = 0
    for ref in refs[:-1]:
        refs[-1][row : row + ref.shape[0], :] = ref[...]
        row += ref.shape[0]


def join(parts, name, after=(), cost=NONE):
    total = jax.ShapeDtypeStruct((sum(p.shape[0] for p in parts), parts[0].shape[1]), BF)
    return run(join_kernel, tuple(parts), (total,), name, cost, scalars=0, after=after)[0]


def place_kernel(rows, bits, idx, *refs):
    q = 0
    for ref in refs[:-1]:
        for row in range(0, ref.shape[0], rows):
            owner = idx[0] ^ int(f"{q:0{bits}b}"[::-1], 2)
            refs[-1][pl.ds(pl.multiple_of(owner * rows, rows), rows), :] = ref[row : row + rows, :]
            q += 1


def fold_kernel(count, *refs):
    total = refs[0][...].astype(F32)
    for ref in refs[1:count]:
        total = total + ref[...].astype(F32)
    total = total.astype(BF)
    row = 0
    for out in refs[count:]:
        out[...] = total[row : row + out.shape[0]]
        row += out.shape[0]


def fold(parts, name, split=1, after=(), cost=NONE):
    rows, columns = parts[0].shape
    out = jax.ShapeDtypeStruct((rows // split, columns), BF)
    kernel = functools.partial(fold_kernel, len(parts))
    return run(kernel, tuple(parts), (out,) * split, name, cost, scalars=0, after=after)


def add(a, b):
    return (a.astype(F32) + b.astype(F32)).astype(BF)


def over_pairs(share):
    pairs = lax.axis_size("space") // 2
    step = 1
    while step < pairs:
        share = add(share, trade(share, "space", 2 * step))
        step *= 2
    return share


def with_halo(t3):
    size = lax.axis_size("space")
    if size == 2:
        return t3
    last = t3.shape[1] - 1
    before = lax.ppermute(t3[:, last - 1], "space", [(i, i + 2) for i in range(size - 2)])
    after = lax.ppermute(t3[:, 1], "space", [(i + 2, i) for i in range(size - 2)])
    return t3.at[:, 0].set(before).at[:, last].set(after)


def body(volumes, cotangent, first_weight, second_weight, first_noise, second_noise):
    _, slab, height, width, channels = volumes.shape
    area = height * width
    hid = channels // 2
    devices = lax.axis_size("dp")
    members = lax.axis_size("space")
    rows = channels // devices
    half = rows // 2
    bits = devices.bit_length() - 1
    dims = (slab, width, area, rows, bits)
    halo = members > 2
    planes = 2 * slab
    cells = planes * area
    idx = jnp.stack([lax.axis_index("dp"), lax.axis_index("space") % 2]).astype(jnp.int32)
    volume = volumes.reshape(slab, area, channels)
    upstream = cotangent.reshape(slab, area, channels)
    shape = jax.ShapeDtypeStruct

    def padded(count):
        return shape((3, planes + 2, area + 2 * width, count), BF)

    core, near, line, far = 1, 2, 4, 8

    other_volume = trade(volume, "space", 1)
    (w1,) = run(
        functools.partial(first_columns_kernel, half),
        (idx, first_weight),
        (shape((rows, 27 * hid), BF),),
        "first_columns",
        NONE,
    )
    w1 = join((w1, trade(w1, "dp", far)), "join1")
    (w2,) = run(
        functools.partial(second_rows_kernel, half),
        (idx, second_weight),
        (shape((half, 27 * channels), BF),),
        "second_rows",
        SHORTER,
        after=(w1,),
    )
    line1, near1 = trade(w1, "dp", line), trade(w1, "dp", near)
    w1 = join((w1, line1, near1), "join1", after=(w2,))
    both1 = trade(line1, "dp", near)
    far2 = trade(w2, "dp", far)
    x3, xt = run(
        functools.partial(spread_kernel, dims, True),
        (idx, volume, other_volume),
        (padded(channels), shape((channels, cells), BF)),
        "spread_volumes",
        ALL,
        after=(w1,),
    )
    x3 = with_halo(x3)
    sum_of = shape(first_weight.shape, F32)
    (base1,) = run(base_kernel, (first_weight, first_noise), (sum_of,), "base1", NONE, scalars=0, after=(xt,))
    w1 = join((w1, both1), "join1", after=(base1,))
    core1 = trade(w1, "dp", core)
    w2 = join((w2, far2), "join2", after=(w1,), cost=ALL)
    line2, near2 = trade(w2, "dp", line), trade(w2, "dp", near)
    (w1,) = run(
        functools.partial(place_kernel, rows, bits),
        (idx, w1, core1),
        (shape((channels, 27 * hid), BF),),
        "place1",
        NONE,
        after=(w2,),
    )
    scratch = [pltpu.VMEM((planes + 2, area, 3 * hid), F32)]
    a3, at, slope = run(
        functools.partial(hidden_kernel, dims, halo),
        (idx, x3, w1),
        (padded(hid), shape((hid, cells), BF), shape((planes, area, hid), BF)),
        "hidden",
        SHORTER,
        scratch=scratch,
    )
    a3 = with_halo(a3)

    w2 = join((w2, line2, near2), "join2", after=(slope,))
    line2 = join((line2,), "join2", after=(slope,))
    both2 = trade(line2, "dp", near)
    other_upstream = trade(upstream, "space", 1)
    (c3,) = run(
        functools.partial(spread_kernel, dims, False),
        (idx, upstream, other_upstream),
        (padded(channels),),
        "spread_cotangent",
        ALL,
        after=(w2,),
    )
    c3 = with_halo(c3)
    keep2, send2 = run(
        functools.partial(second_grad_kernel, dims),
        (at, c3),
        (shape((hid // 2, 27 * channels), BF),) * 2,
        "second_grad",
        NONE,
        scalars=0,
    )
    w2 = join((w2, both2), "join2", after=(keep2,), cost=ALL)
    core2 = trade(w2, "dp", core)
    q01, q23, q45, q67 = fold((keep2, trade(send2, "dp", core)), "fold2", split=4, after=(w2,), cost=ALL)
    w2 = join((w2, core2), "join2", after=(q01,))
    (g3,) = run(
        functools.partial(hidden_grad_kernel, dims, halo),
        (idx, c3, w2, slope),
        (padded(hid),),
        "hidden_grad",
        ALL,
        scratch=scratch,
    )
    g3 = with_halo(g3)

    (q23,) = fold((q23, trade(q67, "dp", near)), "fold2", after=(g3,))
    line2, near2 = trade(q23, "dp", line), trade(join((q45,), "join2", after=(g3,)), "dp", near)
    part, whole = shape((slab, area, channels), BF), shape((slab, area, channels), F32)
    (send_out,) = run(
        functools.partial(outputs_kernel, dims, False), (idx, a3, w2), (part,), "outputs_send", ALL, after=(q23,)
    )
    came_out = trade(send_out, "space", 1)
    keep1, send1 = run(
        functools.partial(first_grad_kernel, dims),
        (xt, g3),
        (shape((channels // 2, 27 * hid), BF),) * 2,
        "first_grad",
        NONE,
        scalars=0,
        after=(send_out,),
    )
    q0, q1 = fold((q01, line2, near2), "fold2", split=2, after=(keep1,), cost=ALL)
    p01, p23, p45, p67 = fold((keep1, trade(send1, "dp", core)), "fold1", split=4, after=(q0,))
    near1 = trade(p67, "dp", near)
    (send_in,) = run(
        functools.partial(input_grads_kernel, dims, False), (idx, g3, w1), (part,), "input_grads_send", ALL, after=(p01,)
    )
    came_in = trade(send_in, "space", 1)
    (p23,) = fold((p23, near1), "fold1", after=(send_in,))
    line1, near1 = trade(p23, "dp", line), trade(join((p45,), "join1", after=(p23,)), "dp", near)
    far2 = trade(q1, "dp", far)
    (own_out,) = run(
        functools.partial(outputs_kernel, dims, True), (idx, a3, w2, volume), (whole,), "outputs", ALL, after=(p23,)
    )
    p0, p1 = fold((p01, line1, near1), "fold1", split=2, after=(own_out,))
    (own_in,) = run(
        functools.partial(input_grads_kernel, dims, True),
        (idx, g3, w1, upstream),
        (whole,),
        "input_grads",
        SHORTER,
        after=(p0,),
    )
    (share2,) = fold((q0, far2), "fold2", after=(own_in,))
    share2 = over_pairs(share2)
    other2 = trade(share2, "space", 1)
    (base2,) = run(base_kernel, (second_weight, second_noise), (sum_of,), "base2", NONE, scalars=0, after=(share2,))
    (outputs,) = run(finish_kernel, (own_out, came_out), (part,), "finish", NONE, scalars=0, after=(base2,))
    (input_grads,) = run(finish_kernel, (own_in, came_in), (part,), "finish", NONE, scalars=0, after=(outputs,))
    (share1,) = fold((p0, trade(p1, "dp", far)), "fold1", after=(input_grads,))
    share1 = over_pairs(share1)
    other1 = trade(share1, "space", 1)
    rate = 1.0 / math.sqrt(slab * area * devices * members)
    (new_second,) = run(
        functools.partial(update_second_kernel, half, rate),
        (idx, share2, other2, base2),
        (sum_of,),
        "update_second",
        NONE,
        after=(share1,),
    )
    (new_first,) = run(
        functools.partial(update_first_kernel, half, rate),
        (idx, share1, other1, base1),
        (sum_of,),
        "update_first",
        NONE,
        after=(new_second,),
    )
    return (outputs.reshape(volumes.shape), input_grads.reshape(volumes.shape), new_first, new_second)


def solution(mesh):
    cells = P("dp", "space", None, None, None)
    rows = P("dp", None)
    return jax.shard_map(
        body,
        mesh=mesh,
        in_specs=(cells, cells, rows, rows, rows, rows),
        out_specs=(cells, cells, rows, rows),
        check_vma=False,
    )
```

```python
import functools
import math

import jax
import jax.numpy as jnp
from jax import lax
from jax.experimental import pallas as pl
from jax.experimental.pallas import tpu as pltpu
from jax.sharding import PartitionSpec as P

NOISE_COEF = 0.25
BF = jnp.bfloat16
F32 = jnp.float32
SPARE, SPARE_HEAVY = 2**20, 5 * 2**20
NONE, SHORTER, ALL = 1, 10**10, 10**11


def dot(a, b):
    return jnp.dot(a, b, preferred_element_type=F32)


def dot_nt(a, b):
    return lax.dot_general(a, b, (((1,), (1,)), ((), ())), preferred_element_type=F32)


def over(value, size):
    return value >> (size.bit_length() - 1)


def within(value, size):
    return value & (size - 1)


def reverse_bits(value, bits):
    total = jnp.zeros_like(value)
    for b in range(bits):
        total = total | (((value >> b) & 1) << (bits - 1 - b))
    return total


def relative_matrix(k, size, rows, bits):
    rel = lax.broadcasted_iota(jnp.int32, (size, size), 0)
    nat = lax.broadcasted_iota(jnp.int32, (size, size), 1)
    want = (k ^ reverse_bits(over(rel, rows), bits)) * rows + within(rel, rows)
    return jnp.where(want == nat, 1.0, 0.0).astype(BF)


def member_matrix(h, channels, half):
    chan = lax.broadcasted_iota(jnp.int32, (channels, channels // 2), 0)
    hid = lax.broadcasted_iota(jnp.int32, (channels, channels // 2), 1)
    want = over(hid, half) * (2 * half) + h * half + within(hid, half)
    return jnp.where(want == chan, 1.0, 0.0).astype(BF)


def shift_matrix(cells, width):
    out = lax.broadcasted_iota(jnp.int32, (2 * cells, cells), 0)
    src = lax.broadcasted_iota(jnp.int32, (2 * cells, cells), 1)
    step = jnp.where(out < cells, -1, 1)
    cell = within(out, cells)
    place = within(cell, width) + step
    inside = (place >= 0) & (place < width)
    return jnp.where(inside & (src == cell + step), 1.0, 0.0).astype(BF)


def clear_border(t3, width, area):
    planes = t3.shape[1] - 2
    zero = jnp.zeros((3, planes + 2, width, t3.shape[3]), BF)
    t3[:, :, 0:width, :] = zero
    t3[:, :, width + area : 2 * width + area, :] = zero
    plane = jnp.zeros((3, area, t3.shape[3]), BF)
    t3[:, 0, width : width + area, :] = plane
    t3[:, planes + 1, width : width + area, :] = plane


def store_shifted(t3, plane, value, shifts, width, area):
    both = dot(shifts, value).astype(BF)
    channels = value.shape[1]
    rows = slice(width, width + area)
    t3[0, plane : plane + 2, rows, :] = both[: 2 * area].reshape(2, area, channels)
    t3[1, plane : plane + 2, rows, :] = value.reshape(2, area, channels)
    t3[2, plane : plane + 2, rows, :] = both[2 * area :].reshape(2, area, channels)


def window(t3, c, plane, count, b, width, area):
    block = t3[c, pl.ds(plane, count), b * width : b * width + area, :]
    return block.reshape(count * area, t3.shape[3])


def base_kernel(weight, noise, base):
    base[...] = weight[...] + NOISE_COEF * noise[...]


def second_rows_kernel(half, idx, second, w2):
    w2[...] = jnp.where(idx[1] == 0, second[0:half, :], second[half : 2 * half, :]).astype(BF)


def first_columns_kernel(half, idx, first, w1):
    h = idx[1]
    channels = 2 * w1.shape[1] // 27
    hid = channels // 2
    select = member_matrix(h, channels, half)
    for a in range(3):
        for bc in range(9):
            t = a * 9 + bc
            u = bc * 3 + a
            taps = first[:, t * channels : (t + 1) * channels].astype(BF)
            w1[:, u * hid : (u + 1) * hid] = dot(taps, select).astype(BF)


def spread_kernel(dims, relative, idx, own, other, t3, *rest):
    slab, width, area, rows, bits = dims
    k, h = idx[0], idx[1]
    channels = t3.shape[3]
    clear_border(t3, width, area)
    shifts = shift_matrix(2 * area, width)
    if relative:
        matrix = relative_matrix(k, channels, rows, bits)
    for pair in range(slab):
        plane = 2 * pair
        member, inside = plane // slab, plane % slab
        mine = own[inside : inside + 2].reshape(2 * area, channels)
        theirs = other[inside : inside + 2].reshape(2 * area, channels)
        value = jnp.where(h == member, mine, theirs)
        if relative:
            rest[0][:, plane * area : (plane + 2) * area] = dot_nt(matrix, value).astype(BF)
        store_shifted(t3, plane + 1, value, shifts, width, area)


def planes_of(halo, planes):
    if halo:
        return [(p, 2) for p in range(0, planes + 2, 2)]
    return [(1 + p, planes // 2) for p in range(0, planes, planes // 2)]


def hidden_kernel(dims, halo, idx, x3, w1, a3, at, slope, z):
    slab, width, area, rows, bits = dims
    k = idx[0]
    hid = w1.shape[1] // 27
    planes = 2 * slab
    for plane, count in planes_of(halo, planes):
        total = None
        for b in range(3):
            for c in range(3):
                u = b * 3 + c
                part = dot(window(x3, c, plane, count, b, width, area), w1[:, u * 3 * hid : (u + 1) * 3 * hid])
                total = part if total is None else total + part
        z[plane : plane + count] = total.reshape(count, area, 3 * hid)
    if not halo:
        z[0] = jnp.zeros((area, 3 * hid), F32)
        z[planes + 1] = jnp.zeros((area, 3 * hid), F32)
    clear_border(a3, width, area)
    shifts = shift_matrix(2 * area, width)
    matrix = relative_matrix(k, hid, rows // 2, bits)
    for d in range(0, planes, 2):
        hidden = z[d : d + 2, :, 0:hid] + z[d + 1 : d + 3, :, hid : 2 * hid] + z[d + 2 : d + 4, :, 2 * hid : 3 * hid]
        hidden = hidden.reshape(2 * area, hid)
        sigma = jax.nn.sigmoid(hidden)
        active = (hidden * sigma).astype(BF)
        grad = (sigma * (1.0 + hidden * (1.0 - sigma))).astype(BF)
        at[:, d * area : (d + 2) * area] = dot_nt(matrix, active).astype(BF)
        slope[d : d + 2] = dot_nt(grad, matrix).astype(BF).reshape(2, area, hid)
        store_shifted(a3, d + 1, dot_nt(active, matrix).astype(BF), shifts, width, area)


def second_grad_kernel(dims, at, c3, keep, send):
    slab, width, area, rows, bits = dims
    channels = c3.shape[3]
    half = keep.shape[0]
    for a in range(3):
        for b in range(3):
            for c in range(3):
                t = (a * 3 + b) * 3 + c
                right = window(c3, 2 - c, 2 - a, 2 * slab, 2 - b, width, area)
                value = dot(at[...], right).astype(BF)
                keep[:, t * channels : (t + 1) * channels] = value[:half]
                send[:, t * channels : (t + 1) * channels] = value[half:]


def hidden_grad_kernel(dims, halo, idx, c3, w2, slope, g3, z):
    slab, width, area, rows, bits = dims
    k = idx[0]
    hid = w2.shape[0]
    channels = c3.shape[3]
    planes = 2 * slab
    for plane, count in planes_of(halo, planes):
        total = None
        for b in range(3):
            for c in range(3):
                taps = [(a * 3 + b) * 3 + c for a in range(3)]
                right = jnp.concatenate([w2[:, t * channels : (t + 1) * channels] for t in taps], axis=0)
                part = dot_nt(window(c3, 2 - c, plane, count, 2 - b, width, area), right)
                total = part if total is None else total + part
        z[plane : plane + count] = total.reshape(count, area, 3 * hid)
    if not halo:
        z[0] = jnp.zeros((area, 3 * hid), F32)
        z[planes + 1] = jnp.zeros((area, 3 * hid), F32)
    clear_border(g3, width, area)
    shifts = shift_matrix(2 * area, width)
    matrix = relative_matrix(k, hid, rows // 2, bits)
    for d in range(0, planes, 2):
        grad = z[d + 2 : d + 4, :, 0:hid] + z[d + 1 : d + 3, :, hid : 2 * hid] + z[d : d + 2, :, 2 * hid : 3 * hid]
        grad = grad.reshape(2 * area, hid)
        value = (grad * slope[d : d + 2].reshape(2 * area, hid).astype(F32)).astype(BF)
        store_shifted(g3, d + 1, dot(value, matrix).astype(BF), shifts, width, area)


def first_grad_kernel(dims, xt, g3, keep, send):
    slab, width, area, rows, bits = dims
    hid = g3.shape[3]
    half = keep.shape[0]
    taps = [(a, b, c) for b in range(3) for c in range(3) for a in range(3)]
    for u in range(0, 27, 2):
        blocks = [window(g3, 2 - c, 2 - a, 2 * slab, 2 - b, width, area) for a, b, c in taps[u : u + 2]]
        right = jnp.concatenate(blocks, axis=1)
        value = dot(xt[...], right).astype(BF)
        keep[:, u * hid : (u + len(blocks)) * hid] = value[:half]
        send[:, u * hid : (u + len(blocks)) * hid] = value[half:]


def outputs_kernel(dims, mine, idx, a3, w2, *refs):
    slab, width, area, rows, bits = dims
    channels = w2.shape[1] // 27
    taps = [(a, b, c) for a in range(3) for b in range(3) for c in range(3)]
    start = (idx[1] if mine else 1 - idx[1]) * slab
    total = None
    for t in range(0, 27, 2):
        left = [window(a3, c, start + a, slab, b, width, area) for a, b, c in taps[t : t + 2]]
        right = [w2[:, v * channels : (v + 1) * channels] for v in range(t, t + len(left))]
        part = dot(jnp.concatenate(left, axis=1), jnp.concatenate(right, axis=0))
        total = part if total is None else total + part
    total = total.reshape(slab, area, channels)
    if mine:
        total = refs[0][...].astype(F32) + total
    refs[-1][...] = total.astype(refs[-1].dtype)


def input_grads_kernel(dims, mine, idx, g3, w1, *refs):
    slab, width, area, rows, bits = dims
    hid = w1.shape[1] // 27
    taps = [(a, b, c) for b in range(3) for c in range(3) for a in range(3)]
    start = (idx[1] if mine else 1 - idx[1]) * slab
    total = None
    for u in range(0, 27, 2):
        left = [window(g3, 2 - c, start + 2 - a, slab, 2 - b, width, area) for a, b, c in taps[u : u + 2]]
        part = dot_nt(jnp.concatenate(left, axis=1), w1[:, u * hid : (u + len(left)) * hid])
        total = part if total is None else total + part
    total = total.reshape(slab, area, w1.shape[0])
    if mine:
        total = refs[0][...].astype(F32) + total
    refs[-1][...] = total.astype(refs[-1].dtype)


def update_first_kernel(half, rate, idx, own, other, base, new):
    h = idx[1]
    hid = own.shape[1] // 27
    channels = 2 * hid
    rows = own.shape[0]
    spread = jnp.concatenate([member_matrix(h, channels, half), member_matrix(1 - h, channels, half)], axis=1)
    both = [jnp.concatenate([r[:, u * hid : (u + 1) * hid] for u in range(27)], axis=0) for r in (own, other)]
    grad = dot_nt(jnp.concatenate(both, axis=1), spread)
    for a in range(3):
        for bc in range(9):
            t, u = a * 9 + bc, bc * 3 + a
            cols = slice(t * channels, (t + 1) * channels)
            new[:, cols] = base[:, cols] - rate * grad[u * rows : (u + 1) * rows]


def update_second_kernel(half, rate, idx, own, other, base, new):
    h = idx[1]
    mine = own[...].astype(F32)
    theirs = other[...].astype(F32)
    for member in range(2):
        grad = jnp.where(h == member, mine, theirs)
        rows = slice(member * half, (member + 1) * half)
        new[rows, :] = base[rows, :] - rate * grad


def finish_kernel(own, came, out):
    out[...] = (own[...] + came[...].astype(F32)).astype(BF)


def run(kernel, args, outs, name, cost, scalars=1, scratch=(), after=()):
    moved = sum(math.prod(a.shape) * a.dtype.itemsize for a in (*args, *outs))
    room = moved + sum(math.prod(a.shape) * a.dtype.itemsize for a in scratch)
    smem = pl.BlockSpec(memory_space=pltpu.SMEM)
    vmem = pl.BlockSpec(memory_space=pltpu.VMEM)
    anywhere = pl.BlockSpec(memory_space=pl.ANY)
    count = len(args)

    def entry(*refs):
        kernel(*refs[:count], *refs[count + len(after) :])

    return pl.pallas_call(
        entry,
        out_shape=tuple(outs),
        in_specs=[smem] * scalars + [vmem] * (count - scalars) + [anywhere] * len(after),
        out_specs=tuple([vmem] * len(outs)),
        scratch_shapes=list(scratch),
        compiler_params=pltpu.CompilerParams(vmem_limit_bytes=room + (SPARE if room < 5 * 2**20 else SPARE_HEAVY)),
        cost_estimate=pl.CostEstimate(flops=cost, bytes_accessed=1, transcendentals=0),
        name=name,
    )(*args, *after)


def trade(array, axis, bit):
    size = lax.axis_size(axis)
    return lax.ppermute(array, axis, [(i, i ^ bit) for i in range(size)])


def join_kernel(*refs):
    row = 0
    for ref in refs[:-1]:
        refs[-1][row : row + ref.shape[0], :] = ref[...]
        row += ref.shape[0]


def join(parts, name, after=(), cost=NONE):
    total = jax.ShapeDtypeStruct((sum(p.shape[0] for p in parts), parts[0].shape[1]), BF)
    return run(join_kernel, tuple(parts), (total,), name, cost, scalars=0, after=after)[0]


def place_kernel(rows, bits, idx, *refs):
    q = 0
    for ref in refs[:-1]:
        for row in range(0, ref.shape[0], rows):
            owner = idx[0] ^ int(f"{q:0{bits}b}"[::-1], 2)
            refs[-1][pl.ds(pl.multiple_of(owner * rows, rows), rows), :] = ref[row : row + rows, :]
            q += 1


def fold_kernel(count, *refs):
    total = refs[0][...].astype(F32)
    for ref in refs[1:count]:
        total = total + ref[...].astype(F32)
    total = total.astype(BF)
    row = 0
    for out in refs[count:]:
        out[...] = total[row : row + out.shape[0]]
        row += out.shape[0]


def fold(parts, name, split=1, after=(), cost=NONE):
    rows, columns = parts[0].shape
    out = jax.ShapeDtypeStruct((rows // split, columns), BF)
    kernel = functools.partial(fold_kernel, len(parts))
    return run(kernel, tuple(parts), (out,) * split, name, cost, scalars=0, after=after)


def add(a, b):
    return (a.astype(F32) + b.astype(F32)).astype(BF)


def over_pairs(share):
    pairs = lax.axis_size("space") // 2
    step = 1
    while step < pairs:
        share = add(share, trade(share, "space", 2 * step))
        step *= 2
    return share


def with_halo(t3):
    size = lax.axis_size("space")
    if size == 2:
        return t3
    last = t3.shape[1] - 1
    before = lax.ppermute(t3[:, last - 1], "space", [(i, i + 2) for i in range(size - 2)])
    after = lax.ppermute(t3[:, 1], "space", [(i + 2, i) for i in range(size - 2)])
    return t3.at[:, 0].set(before).at[:, last].set(after)


def body(volumes, cotangent, first_weight, second_weight, first_noise, second_noise):
    _, slab, height, width, channels = volumes.shape
    area = height * width
    hid = channels // 2
    devices = lax.axis_size("dp")
    members = lax.axis_size("space")
    rows = channels // devices
    half = rows // 2
    bits = devices.bit_length() - 1
    dims = (slab, width, area, rows, bits)
    halo = members > 2
    planes = 2 * slab
    cells = planes * area
    idx = jnp.stack([lax.axis_index("dp"), lax.axis_index("space") % 2]).astype(jnp.int32)
    volume = volumes.reshape(slab, area, channels)
    upstream = cotangent.reshape(slab, area, channels)
    shape = jax.ShapeDtypeStruct

    def padded(count):
        return shape((3, planes + 2, area + 2 * width, count), BF)

    core, near, line, far = 1, 2, 4, 8

    other_volume = trade(volume, "space", 1)
    (w1,) = run(
        functools.partial(first_columns_kernel, half),
        (idx, first_weight),
        (shape((rows, 27 * hid), BF),),
        "first_columns",
        NONE,
    )
    w1 = join((w1, trade(w1, "dp", far)), "join1")
    (w2,) = run(
        functools.partial(second_rows_kernel, half),
        (idx, second_weight),
        (shape((half, 27 * channels), BF),),
        "second_rows",
        SHORTER,
        after=(w1,),
    )
    line1, near1 = trade(w1, "dp", line), trade(w1, "dp", near)
    w1 = join((w1, line1, near1), "join1", after=(w2,))
    both1 = trade(line1, "dp", near)
    far2 = trade(w2, "dp", far)
    x3, xt = run(
        functools.partial(spread_kernel, dims, True),
        (idx, volume, other_volume),
        (padded(channels), shape((channels, cells), BF)),
        "spread_volumes",
        ALL,
        after=(w1,),
    )
    x3 = with_halo(x3)
    sum_of = shape(first_weight.shape, F32)
    (base1,) = run(base_kernel, (first_weight, first_noise), (sum_of,), "base1", NONE, scalars=0, after=(xt,))
    w1 = join((w1, both1), "join1", after=(base1,))
    core1 = trade(w1, "dp", core)
    w2 = join((w2, far2), "join2", after=(w1,), cost=ALL)
    line2, near2 = trade(w2, "dp", line), trade(w2, "dp", near)
    (w1,) = run(
        functools.partial(place_kernel, rows, bits),
        (idx, w1, core1),
        (shape((channels, 27 * hid), BF),),
        "place1",
        NONE,
        after=(w2,),
    )
    scratch = [pltpu.VMEM((planes + 2, area, 3 * hid), F32)]
    a3, at, slope = run(
        functools.partial(hidden_kernel, dims, halo),
        (idx, x3, w1),
        (padded(hid), shape((hid, cells), BF), shape((planes, area, hid), BF)),
        "hidden",
        SHORTER,
        scratch=scratch,
    )
    a3 = with_halo(a3)

    w2 = join((w2, line2, near2), "join2", after=(slope,))
    line2 = join((line2,), "join2", after=(slope,))
    both2 = trade(line2, "dp", near)
    other_upstream = trade(upstream, "space", 1)
    (c3,) = run(
        functools.partial(spread_kernel, dims, False),
        (idx, upstream, other_upstream),
        (padded(channels),),
        "spread_cotangent",
        ALL,
        after=(w2,),
    )
    c3 = with_halo(c3)
    keep2, send2 = run(
        functools.partial(second_grad_kernel, dims),
        (at, c3),
        (shape((hid // 2, 27 * channels), BF),) * 2,
        "second_grad",
        NONE,
        scalars=0,
    )
    w2 = join((w2, both2), "join2", after=(keep2,), cost=ALL)
    core2 = trade(w2, "dp", core)
    q01, q23, q45, q67 = fold((keep2, trade(send2, "dp", core)), "fold2", split=4, after=(w2,), cost=ALL)
    w2 = join((w2, core2), "join2", after=(q01,))
    (g3,) = run(
        functools.partial(hidden_grad_kernel, dims, halo),
        (idx, c3, w2, slope),
        (padded(hid),),
        "hidden_grad",
        ALL,
        scratch=scratch,
    )
    g3 = with_halo(g3)

    (q23,) = fold((q23, trade(q67, "dp", near)), "fold2", after=(g3,))
    line2, near2 = trade(q23, "dp", line), trade(join((q45,), "join2", after=(g3,)), "dp", near)
    part, whole = shape((slab, area, channels), BF), shape((slab, area, channels), F32)
    keep1, send1 = run(
        functools.partial(first_grad_kernel, dims),
        (xt, g3),
        (shape((channels // 2, 27 * hid), BF),) * 2,
        "first_grad",
        ALL,
        scalars=0,
        after=(q23,),
    )
    (send_out,) = run(
        functools.partial(outputs_kernel, dims, False), (idx, a3, w2), (part,), "outputs_send", ALL, after=(keep1,)
    )
    came_out = trade(send_out, "space", 1)
    q0, q1 = fold((q01, line2, near2), "fold2", split=2, after=(send_out,))
    p01, p23, p45, p67 = fold((keep1, trade(send1, "dp", core)), "fold1", split=4, after=(q0,))
    near1 = trade(p67, "dp", near)
    (send_in,) = run(
        functools.partial(input_grads_kernel, dims, False), (idx, g3, w1), (part,), "input_grads_send", ALL, after=(p01,)
    )
    came_in = trade(send_in, "space", 1)
    (p23,) = fold((p23, near1), "fold1", after=(send_in,))
    line1, near1 = trade(p23, "dp", line), trade(join((p45,), "join1", after=(p23,)), "dp", near)
    far2 = trade(join((q1,), "join2", after=(p01,)), "dp", far)
    (own_out,) = run(
        functools.partial(outputs_kernel, dims, True), (idx, a3, w2, volume), (whole,), "outputs", ALL, after=(p23,)
    )
    p0, p1 = fold((p01, line1, near1), "fold1", split=2, after=(own_out,))
    (own_in,) = run(
        functools.partial(input_grads_kernel, dims, True),
        (idx, g3, w1, upstream),
        (whole,),
        "input_grads",
        SHORTER,
        after=(p0,),
    )
    (share2,) = fold((q0, far2), "fold2", after=(own_in,))
    share2 = over_pairs(share2)
    other2 = trade(share2, "space", 1)
    (base2,) = run(base_kernel, (second_weight, second_noise), (sum_of,), "base2", NONE, scalars=0, after=(share2,))
    (outputs,) = run(finish_kernel, (own_out, came_out), (part,), "finish", NONE, scalars=0, after=(base2,))
    (input_grads,) = run(finish_kernel, (own_in, came_in), (part,), "finish", NONE, scalars=0, after=(outputs,))
    (share1,) = fold((p0, trade(p1, "dp", far)), "fold1", after=(input_grads,))
    share1 = over_pairs(share1)
    other1 = trade(share1, "space", 1)
    rate = 1.0 / math.sqrt(slab * area * devices * members)
    (new_second,) = run(
        functools.partial(update_second_kernel, half, rate),
        (idx, share2, other2, base2),
        (sum_of,),
        "update_second",
        NONE,
        after=(share1,),
    )
    (new_first,) = run(
        functools.partial(update_first_kernel, half, rate),
        (idx, share1, other1, base1),
        (sum_of,),
        "update_first",
        NONE,
        after=(new_second,),
    )
    return (outputs.reshape(volumes.shape), input_grads.reshape(volumes.shape), new_first, new_second)


def solution(mesh):
    cells = P("dp", "space", None, None, None)
    rows = P("dp", None)
    return jax.shard_map(
        body,
        mesh=mesh,
        in_specs=(cells, cells, rows, rows, rows, rows),
        out_specs=(cells, cells, rows, rows),
        check_vma=False,
    )
```
